32 devices in a mesh: groups: 2 (over x), blk: 16 (over z, y, core).
Axes of the slice: x: 2, y: 2, z: 4, core: 2. Of those that a mesh axis runs over, the one named last changes fastest.
Arguments:
- initial_vectors: bfloat16 [192, 49152], P(('groups', 'blk')), parts along dimension 0, may hold values from -0.02734375 to 0.02734375
- final_vectors: bfloat16 [256, 49152], P(('groups', 'blk')), parts along dimension 0, may hold values from -6 to 6
- dipole: bfloat16 [3, 384, 256, 256], P(None, ('groups', 'blk')), parts along dimension 1, may hold values from -0.375 to 0.375
- block_lengths: int32 [384], P(('groups', 'blk')), parts along dimension 0, may hold values from 128 to 256, as said below
- pair_mask: int32 [192, 128], P(('groups', 'blk')), parts along dimension 0, may hold values 0 or 1
Outputs:
- strengths: float32 [192, 128], P(('groups', 'blk')), parts along dimension 0
The draws below stay inside these ranges and needn't reach their ends.
There are 2 independent parts, one for each index of `groups`. The reference program is written for one: setup_inputs(seed, part) draws one part's arguments, and reference() takes and returns one part's arrays. A program takes and returns all parts, laid end to end along the dimension named above; each array names one. Nothing has to cross between parts.
Inputs may be any that keep to these rules, and one draw needn't show every extreme that they name: `block_lengths`: every block has at least half of its functions live, and the first block of each J pair is full.
All inputs are finite; a program needn't handle non-finite values. No bound on the sum of `pair_mask` on one device may be relied on, other than what follows from the above.
Results may differ from the reference program's by a relative error of at most 0.0026.
Values may be sent and summed in bfloat16 or wider, within the bound.
A program may use at most 64 MiB of HBM per device.

```python
import jax
import jax.numpy as jnp
from jax import lax

BS = 256
NBLK = 192
NB = 49152
NI = 96
NF = 128


def draw_block_lengths(key, part):
    key = jax.random.fold_in(key, 11)
    values = jax.random.randint(key, (NBLK,), BS // 2, BS + 1, dtype=jnp.int32)
    return values.at[0].set(BS)


def with_ends(values, key, low, top_value):
    longest = values.shape.index(max(values.shape))
    spots = []
    for shift in (0, 1):
        where = [jax.random.randint(jax.random.fold_in(key, axis), (), 0, length) for axis, length in enumerate(values.shape)]
        where[longest] = (where[longest] + shift) % values.shape[longest]
        spots.append(tuple(where))
    return values.at[spots[0]].set(low).at[spots[1]].set(top_value)


def level_of(stream_key, dims, cuts, low, high):
    level, own = 1.0, jax.random.fold_in(stream_key, 6)
    for axis_at, parts in cuts:
        steps = jnp.exp(jax.random.uniform(jax.random.fold_in(own, axis_at), (parts,), jnp.float32, low / len(cuts), high / len(cuts)))
        level = level * jnp.repeat(steps, dims[axis_at] // parts).reshape([-1 if axis == axis_at else 1 for axis in range(len(dims))])
    return level


def centred(rng, dims, width, bound, shards=(), held_as=jnp.bfloat16):
    drawn = jax.random.normal(rng, dims, jnp.float32) * width
    if len(shards) > 0:
        drawn = level_of(rng, dims, shards, -0.22, 0.18) * drawn
    return jnp.clip(drawn, min=-bound, max=bound).astype(held_as)


def setup_inputs(seed: int = 0, part: int = 0) -> dict:
    key_list = jax.random.split(jax.random.key(seed), 6)
    part_splits = jax.random.split(jax.random.fold_in(key_list[5], part), 6)
    return {
        "initial_vectors": centred(part_splits[0], (NI, NB), NB ** -0.5, 0.02734375, ((0, 16),)),
        "final_vectors": centred(part_splits[1], (NF, NB), 1.0, 6.0, ((0, 16),)),
        "dipole": centred(part_splits[2], (3, NBLK, BS, BS), BS ** -0.5, 0.375, ((1, 16),)),
        "block_lengths": draw_block_lengths(jax.random.fold_in(jax.random.fold_in(key_list[5], part), 71), part),
        "pair_mask": with_ends((jax.random.randint(part_splits[4], (NI, NF), 0, 2) < 1).astype(jnp.int32), jax.random.fold_in(part_splits[4], 1), 0, 1),
    }


def reference(initial_vectors, final_vectors, dipole, block_lengths, pair_mask):
    alive = jnp.arange(BS, dtype=jnp.int32)[None, :] < block_lengths[:, None]
    initial_blocks = jnp.transpose(initial_vectors.reshape(NI, NBLK, BS), (1, 2, 0))
    final_blocks = jnp.transpose(final_vectors.reshape(NF, NBLK, BS), (1, 2, 0))
    dipole_blocks = jnp.moveaxis(dipole, 1, 0)

    def accumulate(total, items):
        dipole_tile, initial_rows, final_rows, live_rows = items
        final_rows = jnp.where(live_rows[:, None], final_rows, jnp.zeros_like(final_rows))
        initial_rows = jnp.where(live_rows[:, None], initial_rows, jnp.zeros_like(initial_rows))
        half = jnp.einsum("ckl,lf->ckf", dipole_tile.astype(jnp.float32), final_rows.astype(jnp.float32)).astype(jnp.bfloat16)
        total = total + jnp.einsum("ki,ckf->icf", initial_rows.astype(jnp.float32), half.astype(jnp.float32))
        return total, None

    start_total = jnp.zeros((NI, 3, NF), jnp.float32)
    moments, _ = lax.scan(accumulate, start_total, (dipole_blocks, initial_blocks, final_blocks, alive))
    return pair_mask.astype(jnp.float32) * jnp.sum(moments * moments, axis=1)
```

```python
import functools

import jax
import jax.numpy as jnp
from jax import lax
from jax.experimental import pallas as pl
from jax.experimental.pallas import tpu as pltpu
from jax.sharding import PartitionSpec as P

MESH = pl.DeviceIdType.MESH


def kernel(
    n, chunks,
    initial, final, dipole, lengths, mask, out,
    final_in, initial_in, tiles, partial, arrived,
    tile_sem, send_sem, final_sem, initial_sem, moment_send, moment_recv,
):
    me = lax.axis_index("blk")
    components, blocks, size, _ = dipole.shape
    per_chunk = blocks // chunks
    width = per_chunk * size
    owned, owned_final = initial.shape[0], final.shape[0]
    padded = partial.shape[1]

    tile_copy = pltpu.make_async_copy(dipole, tiles, tile_sem)
    tile_copy.start()

    def columns(owner, chunk):
        return pl.ds(pl.multiple_of(owner * (blocks * size) + chunk * width, size), width)

    for chunk in range(chunks):
        pltpu.make_async_copy(
            final.at[:, columns(me, chunk)], final_in.at[chunk, me], final_sem.at[chunk]
        ).start()
        pltpu.make_async_copy(
            initial.at[:, columns(me, chunk)], initial_in.at[chunk, me], initial_sem.at[chunk]
        ).start()

    barrier = pltpu.get_barrier_semaphore()

    def greet(step, carry):
        pl.semaphore_signal(
            barrier, inc=1, device_id={"blk": lax.rem(me + step, n)}, device_id_type=MESH
        )
        return carry

    lax.fori_loop(1, n, greet, 0)
    pl.semaphore_wait(barrier, n - 1)

    for chunk in range(chunks):

        def send(step, carry):
            peer = lax.rem(me + step, n)
            pltpu.make_async_remote_copy(
                final.at[:, columns(peer, chunk)], final_in.at[chunk, me],
                send_sem.at[0, chunk], final_sem.at[chunk],
                device_id={"blk": peer}, device_id_type=MESH,
            ).start()
            pltpu.make_async_remote_copy(
                initial.at[:, columns(peer, chunk)], initial_in.at[chunk, me],
                send_sem.at[1, chunk], initial_sem.at[chunk],
                device_id={"blk": peer}, device_id_type=MESH,
            ).start()
            return carry

        lax.fori_loop(1, n, send, 0)

    tile_copy.wait()
    total = [jnp.zeros((n * padded, n * owned_final), jnp.float32)] * components
    for chunk in range(chunks):
        pltpu.make_async_copy(final_in.at[chunk], final_in.at[chunk], final_sem.at[chunk]).wait()
        pltpu.make_async_copy(initial_in.at[chunk], initial_in.at[chunk], initial_sem.at[chunk]).wait()
        for j in range(per_chunk):
            block = chunk * per_chunk + j
            alive = lax.broadcasted_iota(jnp.int32, (1, 1, size), 2) < lengths[block]
            finals = final_in[chunk, :, :, j * size : (j + 1) * size].astype(jnp.float32)
            finals = jnp.where(alive, finals, 0.0).reshape(n * owned_final, size).astype(jnp.bfloat16)
            initials = initial_in[chunk, :, :, j * size : (j + 1) * size].astype(jnp.float32)
            initials = jnp.where(alive, initials, 0.0)
            if padded > owned:
                initials = jnp.concatenate(
                    [initials, jnp.zeros((n, padded - owned, size), jnp.float32)], axis=1
                )
            initials = initials.reshape(n * padded, size).astype(jnp.bfloat16)
            half = lax.dot_general(
                tiles[:, block].reshape(components * size, size), finals,
                (((1,), (1,)), ((), ())), preferred_element_type=jnp.float32,
            ).astype(jnp.bfloat16)
            for c in range(components):
                total[c] = total[c] + jnp.dot(
                    initials, half[c * size : (c + 1) * size], preferred_element_type=jnp.float32
                )
    finals_all = n * owned_final
    for c in range(components):
        partial[:, :, c * finals_all : (c + 1) * finals_all] = total[c].reshape(n, padded, finals_all)

    def spread(step, carry):
        peer = lax.rem(me + step, n)
        pltpu.make_async_remote_copy(
            partial.at[peer], arrived.at[me], moment_send, moment_recv,
            device_id={"blk": peer}, device_id_type=MESH,
        ).start()
        return carry

    lax.fori_loop(1, n, spread, 0)
    pltpu.make_async_copy(partial.at[me], arrived.at[me], moment_recv).start()
    pltpu.make_async_copy(arrived, arrived, moment_recv).wait()
    moments = jnp.sum(arrived[...], axis=0)
    squares = moments * moments
    strength = squares[:, :finals_all]
    for c in range(1, components):
        strength = strength + squares[:, c * finals_all : (c + 1) * finals_all]
    out[...] = mask[...].astype(jnp.float32) * strength[:owned]

    for chunk in range(chunks):
        pltpu.make_async_copy(
            final_in.at[chunk, pl.ds(0, n - 1)], final_in.at[chunk, pl.ds(0, n - 1)], send_sem.at[0, chunk]
        ).wait()
        pltpu.make_async_copy(
            initial_in.at[chunk, pl.ds(0, n - 1)], initial_in.at[chunk, pl.ds(0, n - 1)], send_sem.at[1, chunk]
        ).wait()
    pltpu.make_async_copy(
        partial.at[pl.ds(0, n - 1)], partial.at[pl.ds(0, n - 1)], moment_send
    ).wait()


def on_device(n, initial_vectors, final_vectors, dipole, block_lengths, pair_mask):
    components, blocks, size, _ = dipole.shape
    owned, owned_final = initial_vectors.shape[0], final_vectors.shape[0]
    chunks = 4
    width = blocks // chunks * size
    padded = -(-owned // 8) * 8
    return pl.pallas_call(
        functools.partial(kernel, n, chunks),
        out_shape=jax.ShapeDtypeStruct(pair_mask.shape, jnp.float32),
        in_specs=[
            pl.BlockSpec(memory_space=pl.ANY),
            pl.BlockSpec(memory_space=pl.ANY),
            pl.BlockSpec(memory_space=pl.ANY),
            pl.BlockSpec(memory_space=pltpu.SMEM),
            pl.BlockSpec(memory_space=pltpu.VMEM),
        ],
        out_specs=pl.BlockSpec(memory_space=pltpu.VMEM),
        scratch_shapes=[
            pltpu.VMEM((chunks, n, owned_final, width), jnp.bfloat16),
            pltpu.VMEM((chunks, n, owned, width), jnp.bfloat16),
            pltpu.VMEM(dipole.shape, jnp.bfloat16),
            pltpu.VMEM((n, padded, components * n * owned_final), jnp.float32),
            pltpu.VMEM((n, padded, components * n * owned_final), jnp.float32),
            pltpu.SemaphoreType.DMA,
            pltpu.SemaphoreType.DMA((2, chunks)),
            pltpu.SemaphoreType.DMA((chunks,)),
            pltpu.SemaphoreType.DMA((chunks,)),
            pltpu.SemaphoreType.DMA,
            pltpu.SemaphoreType.DMA,
        ],
        compiler_params=pltpu.CompilerParams(
            collective_id=0, has_side_effects=True, vmem_limit_bytes=56 * 1024 * 1024
        ),
        cost_estimate=pl.CostEstimate(
            flops=2 * components * blocks * size * n * owned_final * (size + n * padded),
            bytes_accessed=2 * components * blocks * size * size + 4 * n * width * chunks * owned_final,
            transcendentals=0,
        ),
    )(initial_vectors, final_vectors, dipole, block_lengths, pair_mask)


def solution(mesh):
    placed = (
        P(("groups", "blk"), None),
        P(("groups", "blk"), None),
        P(None, ("groups", "blk"), None, None),
        P(("groups", "blk")),
        P(("groups", "blk"), None),
    )
    return jax.shard_map(
        functools.partial(on_device, mesh.shape["blk"]),
        mesh=mesh, in_specs=placed, out_specs=P(("groups", "blk"), None), check_vma=False,
    )
```

```python
import functools

import jax
import jax.numpy as jnp
from jax import lax
from jax.experimental import pallas as pl
from jax.experimental.pallas import tpu as pltpu
from jax.sharding import PartitionSpec as P

MESH = pl.DeviceIdType.MESH


def kernel(
    n, chunks,
    initial, final, dipole, lengths, mask, out,
    staged, packed, final_in, initial_in, tiles, partial, arrived,
    stage_sem, tile_sem, send_sem, final_sem, initial_sem, moment_send, moment_recv,
):
    me = lax.axis_index("blk")
    components, blocks, size, _ = dipole.shape
    per_chunk = blocks // chunks
    width = per_chunk * size
    owned, owned_final = initial.shape[0], final.shape[0]
    padded = partial.shape[1]
    spare = padded - owned
    full = chunks - 1

    stage_copy = pltpu.make_async_copy(initial, staged, stage_sem)
    stage_copy.start()
    tile_copy = pltpu.make_async_copy(dipole, tiles, tile_sem)
    tile_copy.start()

    def columns(owner, chunk):
        return pl.ds(pl.multiple_of(owner * (blocks * size) + chunk * width, size), width)

    for chunk in range(chunks):
        pltpu.make_async_copy(
            final.at[:, columns(me, chunk)], final_in.at[chunk, me], final_sem.at[chunk]
        ).start()

    barrier = pltpu.get_barrier_semaphore()

    def greet(step, carry):
        pl.semaphore_signal(
            barrier, inc=1, device_id={"blk": lax.rem(me + step, n)}, device_id_type=MESH
        )
        return carry

    lax.fori_loop(1, n, greet, 0)

    stage_copy.wait()

    def pack(owner, carry):
        start = pl.multiple_of(owner * (blocks * size), blocks * size)
        rows = staged[:, pl.ds(start, blocks * size)].astype(jnp.float32)
        last = rows[:, full * width :]
        for chunk in range(full):
            packed[owner, chunk] = jnp.concatenate(
                [rows[:, chunk * width : (chunk + 1) * width]]
                + [last[chunk + e * full : chunk + e * full + 1] for e in range(spare)],
                axis=0,
            ).astype(jnp.bfloat16)
        return carry

    lax.fori_loop(0, n, pack, 0)
    for chunk in range(full):
        pltpu.make_async_copy(
            packed.at[me, chunk], initial_in.at[chunk, me], initial_sem.at[chunk]
        ).start()
    pl.semaphore_wait(barrier, n - 1)

    for chunk in range(chunks):

        def send(step, carry):
            peer = lax.rem(me + step, n)
            pltpu.make_async_remote_copy(
                final.at[:, columns(peer, chunk)], final_in.at[chunk, me],
                send_sem.at[0, chunk], final_sem.at[chunk],
                device_id={"blk": peer}, device_id_type=MESH,
            ).start()
            if chunk < full:
                pltpu.make_async_remote_copy(
                    packed.at[peer, chunk], initial_in.at[chunk, me],
                    send_sem.at[1, chunk], initial_sem.at[chunk],
                    device_id={"blk": peer}, device_id_type=MESH,
                ).start()
            return carry

        lax.fori_loop(1, n, send, 0)

    tile_copy.wait()
    total = [jnp.zeros((n * padded, n * owned_final), jnp.float32)] * components
    for chunk in range(chunks):
        pltpu.make_async_copy(final_in.at[chunk], final_in.at[chunk], final_sem.at[chunk]).wait()
        if chunk < full:
            pltpu.make_async_copy(initial_in.at[chunk], initial_in.at[chunk], initial_sem.at[chunk]).wait()
        for j in range(per_chunk):
            block = chunk * per_chunk + j
            alive = lax.broadcasted_iota(jnp.int32, (1, 1, size), 2) < lengths[block]
            finals = final_in[chunk, :, :, j * size : (j + 1) * size].astype(jnp.float32)
            finals = jnp.where(alive, finals, 0.0).reshape(n * owned_final, size).astype(jnp.bfloat16)
            place = slice(j * size, (j + 1) * size)
            if chunk < full:
                initials = initial_in[chunk, :, :, place].astype(jnp.float32)
            else:
                carried = [
                    initial_in[g, :, owned:, place].astype(jnp.float32) for g in range(full)
                ]
                initials = jnp.concatenate(
                    [carried[r % full][:, r // full : r // full + 1] for r in range(owned)]
                    + [jnp.zeros((n, spare, size), jnp.float32)],
                    axis=1,
                )
            initials = jnp.where(alive, initials, 0.0)
            initials = initials.reshape(n * padded, size).astype(jnp.bfloat16)
            half = lax.dot_general(
                tiles[:, block].reshape(components * size, size), finals,
                (((1,), (1,)), ((), ())), preferred_element_type=jnp.float32,
            ).astype(jnp.bfloat16)
            for c in range(components):
                total[c] = total[c] + jnp.dot(
                    initials, half[c * size : (c + 1) * size], preferred_element_type=jnp.float32
                )
    finals_all = n * owned_final
    for c in range(components):
        partial[:, :, c * finals_all : (c + 1) * finals_all] = total[c].reshape(n, padded, finals_all)

    def spread(step, carry):
        peer = lax.rem(me + step, n)
        pltpu.make_async_remote_copy(
            partial.at[peer], arrived.at[me], moment_send, moment_recv,
            device_id={"blk": peer}, device_id_type=MESH,
        ).start()
        return carry

    lax.fori_loop(1, n, spread, 0)
    pltpu.make_async_copy(partial.at[me], arrived.at[me], moment_recv).start()
    pltpu.make_async_copy(arrived, arrived, moment_recv).wait()
    moments = jnp.sum(arrived[...], axis=0)
    squares = moments * moments
    strength = squares[:, :finals_all]
    for c in range(1, components):
        strength = strength + squares[:, c * finals_all : (c + 1) * finals_all]
    out[...] = mask[...].astype(jnp.float32) * strength[:owned]

    for chunk in range(chunks):
        pltpu.make_async_copy(
            final_in.at[chunk, pl.ds(0, n - 1)], final_in.at[chunk, pl.ds(0, n - 1)], send_sem.at[0, chunk]
        ).wait()
        if chunk < full:
            pltpu.make_async_copy(
                initial_in.at[chunk, pl.ds(0, n - 1)], initial_in.at[chunk, pl.ds(0, n - 1)], send_sem.at[1, chunk]
            ).wait()
    pltpu.make_async_copy(
        partial.at[pl.ds(0, n - 1)], partial.at[pl.ds(0, n - 1)], moment_send
    ).wait()


def on_device(n, initial_vectors, final_vectors, dipole, block_lengths, pair_mask):
    components, blocks, size, _ = dipole.shape
    owned, owned_final = initial_vectors.shape[0], final_vectors.shape[0]
    padded = (owned // 8 + 1) * 8
    full = -(-owned // (padded - owned))
    chunks = full + 1
    assert blocks % chunks == 0 and full * (padded - owned) == owned
    width = blocks // chunks * size
    return pl.pallas_call(
        functools.partial(kernel, n, chunks),
        out_shape=jax.ShapeDtypeStruct(pair_mask.shape, jnp.float32),
        in_specs=[
            pl.BlockSpec(memory_space=pl.ANY),
            pl.BlockSpec(memory_space=pl.ANY),
            pl.BlockSpec(memory_space=pl.ANY),
            pl.BlockSpec(memory_space=pltpu.SMEM),
            pl.BlockSpec(memory_space=pltpu.VMEM),
        ],
        out_specs=pl.BlockSpec(memory_space=pltpu.VMEM),
        scratch_shapes=[
            pltpu.VMEM(initial_vectors.shape, jnp.bfloat16),
            pltpu.VMEM((n, full, padded, width), jnp.bfloat16),
            pltpu.VMEM((chunks, n, owned_final, width), jnp.bfloat16),
            pltpu.VMEM((full, n, padded, width), jnp.bfloat16),
            pltpu.VMEM(dipole.shape, jnp.bfloat16),
            pltpu.VMEM((n, padded, components * n * owned_final), jnp.float32),
            pltpu.VMEM((n, padded, components * n * owned_final), jnp.float32),
            pltpu.SemaphoreType.DMA,
            pltpu.SemaphoreType.DMA,
            pltpu.SemaphoreType.DMA((2, chunks)),
            pltpu.SemaphoreType.DMA((chunks,)),
            pltpu.SemaphoreType.DMA((chunks,)),
            pltpu.SemaphoreType.DMA,
            pltpu.SemaphoreType.DMA,
        ],
        compiler_params=pltpu.CompilerParams(
            collective_id=0, has_side_effects=True, vmem_limit_bytes=56 * 1024 * 1024
        ),
        cost_estimate=pl.CostEstimate(
            flops=2 * components * blocks * size * n * owned_final * (size + n * padded),
            bytes_accessed=2 * components * blocks * size * size + 4 * n * width * chunks * owned_final,
            transcendentals=0,
        ),
    )(initial_vectors, final_vectors, dipole, block_lengths, pair_mask)


def solution(mesh):
    placed = (
        P(("groups", "blk"), None),
        P(("groups", "blk"), None),
        P(None, ("groups", "blk"), None, None),
        P(("groups", "blk")),
        P(("groups", "blk"), None),
    )
    return jax.shard_map(
        functools.partial(on_device, mesh.shape["blk"]),
        mesh=mesh, in_specs=placed, out_specs=P(("groups", "blk"), None), check_vma=False,
    )
```

```python
import functools

import jax
import jax.numpy as jnp
from jax import lax
from jax.experimental import pallas as pl
from jax.experimental.pallas import tpu as pltpu
from jax.sharding import PartitionSpec as P

MESH = pl.DeviceIdType.MESH


def kernel(
    n, chunks,
    initial, final, dipole, lengths, mask, out,
    staged, packed, final_in, initial_in, tiles, partial, arrived,
    stage_sem, tile_sem, send_sem, final_sem, initial_sem, moment_send, moment_recv, passed,
):
    me = lax.axis_index("blk")
    components, blocks, size, _ = dipole.shape
    per_chunk = blocks // chunks
    width = per_chunk * size
    owned, owned_final = initial.shape[0], final.shape[0]
    padded = packed.shape[2]
    spare = padded - owned
    full = chunks - 1

    stage_copy = pltpu.make_async_copy(initial, staged, stage_sem)
    stage_copy.start()
    tile_copy = pltpu.make_async_copy(dipole, tiles, tile_sem)
    tile_copy.start()

    def columns(owner, chunk):
        return pl.ds(pl.multiple_of(owner * (blocks * size) + chunk * width, size), width)

    for chunk in range(chunks):
        pltpu.make_async_copy(
            final.at[:, columns(me, chunk)], final_in.at[chunk, me], final_sem.at[chunk]
        ).start()

    barrier = pltpu.get_barrier_semaphore()

    per_quarter = n // 4
    quarter, local = me // per_quarter, lax.rem(me, per_quarter)

    def distance(peer):
        return jnp.abs(peer // per_quarter - quarter)

    def greet(step, carry):
        peer = lax.rem(me + step, n)

        @pl.when(distance(peer) <= 1)
        def _():
            pl.semaphore_signal(barrier, inc=1, device_id={"blk": peer}, device_id_type=MESH)

        return carry

    lax.fori_loop(1, n, greet, 0)

    stage_copy.wait()

    def pack(owner, carry):
        start = pl.multiple_of(owner * (blocks * size), blocks * size)
        rows = staged[:, pl.ds(start, blocks * size)].astype(jnp.float32)
        last = rows[:, full * width :]
        for chunk in range(full):
            packed[owner, chunk] = jnp.concatenate(
                [rows[:, chunk * width : (chunk + 1) * width]]
                + [last[chunk + e * full : chunk + e * full + 1] for e in range(spare)],
                axis=0,
            ).astype(jnp.bfloat16)
        return carry

    lax.fori_loop(0, n, pack, 0)
    for chunk in range(full):
        pltpu.make_async_copy(
            packed.at[me, chunk], initial_in.at[chunk, me], initial_sem.at[chunk]
        ).start()
    inner = (quarter > 0).astype(jnp.int32) + (quarter < 3).astype(jnp.int32)
    pl.semaphore_wait(barrier, per_quarter * (1 + inner) - 1)

    def pass_on(hops):
        for side in (1, -1):
            target = quarter + side
            behind = quarter - side * (hops - 1)

            @pl.when((target >= 0) & (target <= 3) & (behind >= 0) & (behind <= 3))
            def _():
                pl.semaphore_signal(
                    passed.at[hops - 2, (1 - side) // 2], inc=1,
                    device_id={"blk": target * per_quarter + local}, device_id_type=MESH,
                )

        for side in (1, -1):
            source = quarter - side * hops

            @pl.when((source >= 0) & (source <= 3))
            def _():
                pl.semaphore_wait(passed.at[hops - 2, (1 - side) // 2], 1)

    for chunk in range(chunks):

        def send_to(peer):
            pltpu.make_async_remote_copy(
                final.at[:, columns(peer, chunk)], final_in.at[chunk, me],
                send_sem.at[0, chunk], final_sem.at[chunk],
                device_id={"blk": peer}, device_id_type=MESH,
            ).start()
            if chunk < full:
                pltpu.make_async_remote_copy(
                    packed.at[peer, chunk], initial_in.at[chunk, me],
                    send_sem.at[1, chunk], initial_sem.at[chunk],
                    device_id={"blk": peer}, device_id_type=MESH,
                ).start()

        def send(step, carry):
            send_to(lax.rem(me + step, n))
            return carry

        def send_within(low, high):
            def step_to(step, carry):
                peer = lax.rem(me + step, n)

                @pl.when((distance(peer) >= low) & (distance(peer) <= high))
                def _():
                    send_to(peer)

                return carry

            lax.fori_loop(1, n, step_to, 0)

        if chunk == 0:
            send_within(0, 1)
            pass_on(2)
            send_within(2, 2)
            pass_on(3)
            send_within(3, 3)
        else:
            lax.fori_loop(1, n, send, 0)

    tile_copy.wait()
    finals_all = n * owned_final
    total = [jnp.zeros((n * padded, n * owned_final), jnp.float32)] * components
    for chunk in range(chunks):
        pltpu.make_async_copy(final_in.at[chunk], final_in.at[chunk], final_sem.at[chunk]).wait()
        if chunk < full:
            pltpu.make_async_copy(initial_in.at[chunk], initial_in.at[chunk], initial_sem.at[chunk]).wait()
        for j in range(per_chunk):
            block = chunk * per_chunk + j
            alive = lax.broadcasted_iota(jnp.int32, (1, 1, size), 2) < lengths[block]
            finals = final_in[chunk, :, :, j * size : (j + 1) * size].astype(jnp.float32)
            finals = jnp.where(alive, finals, 0.0).reshape(n * owned_final, size).astype(jnp.bfloat16)
            place = slice(j * size, (j + 1) * size)
            if chunk < full:
                initials = initial_in[chunk, :, :, place].astype(jnp.float32)
            else:
                carried = [
                    initial_in[g, :, owned:, place].astype(jnp.float32) for g in range(full)
                ]
                initials = jnp.concatenate(
                    [carried[r % full][:, r // full : r // full + 1] for r in range(owned)]
                    + [jnp.zeros((n, spare, size), jnp.float32)],
                    axis=1,
                )
            initials = jnp.where(alive, initials, 0.0)
            initials = initials.reshape(n * padded, size).astype(jnp.bfloat16)
            half = lax.dot_general(
                tiles[:, block].reshape(components * size, size), finals,
                (((1,), (1,)), ((), ())), preferred_element_type=jnp.float32,
            ).astype(jnp.bfloat16)
            for c in range(components):
                total[c] = total[c] + jnp.dot(
                    initials, half[c * size : (c + 1) * size], preferred_element_type=jnp.float32
                )
    lanes = partial.shape[2]
    pieces = finals_all // lanes
    for c in range(components):
        for p in range(pieces):
            row = (c * pieces + p) * owned
            partial[:, row : row + owned, :] = total[c][:, p * lanes : (p + 1) * lanes].reshape(
                n, padded, lanes
            )[:, :owned]

    def spread(step, carry):
        peer = lax.rem(me + step, n)
        pltpu.make_async_remote_copy(
            partial.at[peer], arrived.at[me], moment_send, moment_recv,
            device_id={"blk": peer}, device_id_type=MESH,
        ).start()
        return carry

    lax.fori_loop(1, n, spread, 0)
    pltpu.make_async_copy(partial.at[me], arrived.at[me], moment_recv).start()
    pltpu.make_async_copy(arrived, arrived, moment_recv).wait()
    moments = jnp.sum(arrived[...], axis=0)
    strengths = []
    for p in range(pieces):
        strength = jnp.zeros((owned, lanes), jnp.float32)
        for c in range(components):
            row = (c * pieces + p) * owned
            strength = strength + moments[row : row + owned] * moments[row : row + owned]
        strengths.append(strength)
    strength = jnp.concatenate(strengths, axis=1)
    out[...] = mask[...].astype(jnp.float32) * strength

    for chunk in range(chunks):
        pltpu.make_async_copy(
            final_in.at[chunk, pl.ds(0, n - 1)], final_in.at[chunk, pl.ds(0, n - 1)], send_sem.at[0, chunk]
        ).wait()
        if chunk < full:
            pltpu.make_async_copy(
                initial_in.at[chunk, pl.ds(0, n - 1)], initial_in.at[chunk, pl.ds(0, n - 1)], send_sem.at[1, chunk]
            ).wait()
    pltpu.make_async_copy(
        partial.at[pl.ds(0, n - 1)], partial.at[pl.ds(0, n - 1)], moment_send
    ).wait()


def on_device(n, initial_vectors, final_vectors, dipole, block_lengths, pair_mask):
    components, blocks, size, _ = dipole.shape
    owned, owned_final = initial_vectors.shape[0], final_vectors.shape[0]
    padded = (owned // 8 + 1) * 8
    full = -(-owned // (padded - owned))
    chunks = full + 1
    assert blocks % chunks == 0 and full * (padded - owned) == owned
    width = blocks // chunks * size
    return pl.pallas_call(
        functools.partial(kernel, n, chunks),
        out_shape=jax.ShapeDtypeStruct(pair_mask.shape, jnp.float32),
        in_specs=[
            pl.BlockSpec(memory_space=pl.ANY),
            pl.BlockSpec(memory_space=pl.ANY),
            pl.BlockSpec(memory_space=pl.ANY),
            pl.BlockSpec(memory_space=pltpu.SMEM),
            pl.BlockSpec(memory_space=pltpu.VMEM),
        ],
        out_specs=pl.BlockSpec(memory_space=pltpu.VMEM),
        scratch_shapes=[
            pltpu.VMEM(initial_vectors.shape, jnp.bfloat16),
            pltpu.VMEM((n, full, padded, width), jnp.bfloat16),
            pltpu.VMEM((chunks, n, owned_final, width), jnp.bfloat16),
            pltpu.VMEM((full, n, padded, width), jnp.bfloat16),
            pltpu.VMEM(dipole.shape, jnp.bfloat16),
            pltpu.VMEM((n, components * (n * owned_final // 128) * owned, 128), jnp.float32),
            pltpu.VMEM((n, components * (n * owned_final // 128) * owned, 128), jnp.float32),
            pltpu.SemaphoreType.DMA,
            pltpu.SemaphoreType.DMA,
            pltpu.SemaphoreType.DMA((2, chunks)),
            pltpu.SemaphoreType.DMA((chunks,)),
            pltpu.SemaphoreType.DMA((chunks,)),
            pltpu.SemaphoreType.DMA,
            pltpu.SemaphoreType.DMA,
            pltpu.SemaphoreType.REGULAR((2, 2)),
        ],
        compiler_params=pltpu.CompilerParams(
            collective_id=0, has_side_effects=True, vmem_limit_bytes=56 * 1024 * 1024
        ),
        cost_estimate=pl.CostEstimate(
            flops=2 * components * blocks * size * n * owned_final * (size + n * padded),
            bytes_accessed=2 * components * blocks * size * size + 4 * n * width * chunks * owned_final,
            transcendentals=0,
        ),
    )(initial_vectors, final_vectors, dipole, block_lengths, pair_mask)


def solution(mesh):
    placed = (
        P(("groups", "blk"), None),
        P(("groups", "blk"), None),
        P(None, ("groups", "blk"), None, None),
        P(("groups", "blk")),
        P(("groups", "blk"), None),
    )
    return jax.shard_map(
        functools.partial(on_device, mesh.shape["blk"]),
        mesh=mesh, in_specs=placed, out_specs=P(("groups", "blk"), None), check_vma=False,
    )
```

```python
import functools

import jax
import jax.numpy as jnp
from jax import lax
from jax.experimental import pallas as pl
from jax.experimental.pallas import tpu as pltpu
from jax.sharding import PartitionSpec as P

MESH = pl.DeviceIdType.MESH


def kernel(
    n, chunks,
    initial, final, dipole, lengths, mask, out,
    staged, packed, final_in, initial_in, tiles, partial, arrived,
    stage_sem, tile_sem, send_sem, final_sem, initial_sem, moment_send, moment_recv, passed,
):
    me = lax.axis_index("blk")
    components, blocks, size, _ = dipole.shape
    per_chunk = blocks // chunks
    width = per_chunk * size
    owned, owned_final = initial.shape[0], final.shape[0]
    padded = packed.shape[2]
    spare = padded - owned
    full = chunks - 1

    stage_copy = pltpu.make_async_copy(initial, staged, stage_sem)
    stage_copy.start()
    tile_copy = pltpu.make_async_copy(dipole, tiles, tile_sem)
    tile_copy.start()

    def columns(owner, chunk):
        return pl.ds(pl.multiple_of(owner * (blocks * size) + chunk * width, size), width)

    for chunk in range(chunks):
        pltpu.make_async_copy(
            final.at[:, columns(me, chunk)], final_in.at[chunk, me], final_sem.at[chunk]
        ).start()

    barrier = pltpu.get_barrier_semaphore()

    per_quarter = n // 4
    quarter, local = me // per_quarter, lax.rem(me, per_quarter)

    def distance(peer):
        return jnp.abs(peer // per_quarter - quarter)

    def greet(step, carry):
        peer = lax.rem(me + step, n)

        @pl.when(distance(peer) <= 1)
        def _():
            pl.semaphore_signal(barrier, inc=1, device_id={"blk": peer}, device_id_type=MESH)

        return carry

    lax.fori_loop(1, n, greet, 0)

    stage_copy.wait()

    def pack(owner, carry):
        start = pl.multiple_of(owner * (blocks * size), blocks * size)
        rows = staged[:, pl.ds(start, blocks * size)].astype(jnp.float32)
        last = rows[:, full * width :]
        for chunk in range(full):
            packed[owner, chunk] = jnp.concatenate(
                [rows[:, chunk * width : (chunk + 1) * width]]
                + [last[chunk + e * full : chunk + e * full + 1] for e in range(spare)],
                axis=0,
            ).astype(jnp.bfloat16)
        return carry

    lax.fori_loop(0, n, pack, 0)
    for chunk in range(full):
        pltpu.make_async_copy(
            packed.at[me, chunk], initial_in.at[chunk, me], initial_sem.at[chunk]
        ).start()
    inner = (quarter > 0).astype(jnp.int32) + (quarter < 3).astype(jnp.int32)
    pl.semaphore_wait(barrier, per_quarter * (1 + inner) - 1)

    def pass_on(hops):
        for side in (1, -1):
            target = quarter + side
            behind = quarter - side * (hops - 1)

            @pl.when((target >= 0) & (target <= 3) & (behind >= 0) & (behind <= 3))
            def _():
                pl.semaphore_signal(
                    passed.at[hops - 2, (1 - side) // 2], inc=1,
                    device_id={"blk": target * per_quarter + local}, device_id_type=MESH,
                )

        for side in (1, -1):
            source = quarter - side * hops

            @pl.when((source >= 0) & (source <= 3))
            def _():
                pl.semaphore_wait(passed.at[hops - 2, (1 - side) // 2], 1)

    for chunk in range(chunks):

        def send_to(peer):
            pltpu.make_async_remote_copy(
                final.at[:, columns(peer, chunk)], final_in.at[chunk, me],
                send_sem.at[0, chunk], final_sem.at[chunk],
                device_id={"blk": peer}, device_id_type=MESH,
            ).start()
            if chunk < full:
                pltpu.make_async_remote_copy(
                    packed.at[peer, chunk], initial_in.at[chunk, me],
                    send_sem.at[1, chunk], initial_sem.at[chunk],
                    device_id={"blk": peer}, device_id_type=MESH,
                ).start()

        def send(step, carry):
            send_to(lax.rem(me + step, n))
            return carry

        def send_within(low, high):
            def step_to(step, carry):
                peer = lax.rem(me + step, n)

                @pl.when((distance(peer) >= low) & (distance(peer) <= high))
                def _():
                    send_to(peer)

                return carry

            lax.fori_loop(1, n, step_to, 0)

        if chunk == 0:
            send_within(0, 1)
            pass_on(2)
            send_within(2, 2)
            pass_on(3)
            send_within(3, 3)
        else:
            lax.fori_loop(1, n, send, 0)

    def live_initials(chunk, j):
        alive = lax.broadcasted_iota(jnp.int32, (1, 1, size), 2) < lengths[chunk * per_chunk + j]
        place = slice(j * size, (j + 1) * size)
        if chunk < full:
            initials = initial_in[chunk, :, :, place].astype(jnp.float32)
        else:
            carried = [
                initial_in[g, :, owned:, place].astype(jnp.float32) for g in range(full)
            ]
            initials = jnp.concatenate(
                [carried[r % full][:, r // full : r // full + 1] for r in range(owned)]
                + [jnp.zeros((n, spare, size), jnp.float32)],
                axis=1,
            )
        initials = jnp.where(alive, initials, 0.0)
        return initials.reshape(n * padded, size).astype(jnp.bfloat16)

    tile_copy.wait()
    finals_all = n * owned_final
    total = [jnp.zeros((n * padded, n * owned_final), jnp.float32)] * components
    for chunk in range(chunks):
        if chunk < full:
            pltpu.make_async_copy(initial_in.at[chunk], initial_in.at[chunk], initial_sem.at[chunk]).wait()
        states = [live_initials(chunk, j) for j in range(per_chunk)]
        pltpu.make_async_copy(final_in.at[chunk], final_in.at[chunk], final_sem.at[chunk]).wait()
        for j in range(per_chunk):
            block = chunk * per_chunk + j
            alive = lax.broadcasted_iota(jnp.int32, (1, 1, size), 2) < lengths[block]
            finals = final_in[chunk, :, :, j * size : (j + 1) * size].astype(jnp.float32)
            finals = jnp.where(alive, finals, 0.0).reshape(n * owned_final, size).astype(jnp.bfloat16)
            initials = states[j]
            half = lax.dot_general(
                tiles[:, block].reshape(components * size, size), finals,
                (((1,), (1,)), ((), ())), preferred_element_type=jnp.float32,
            ).astype(jnp.bfloat16)
            for c in range(components):
                total[c] = total[c] + jnp.dot(
                    initials, half[c * size : (c + 1) * size], preferred_element_type=jnp.float32
                )
    lanes = partial.shape[2]
    pieces = finals_all // lanes
    for c in range(components):
        for p in range(pieces):
            row = (c * pieces + p) * owned
            partial[:, row : row + owned, :] = total[c][:, p * lanes : (p + 1) * lanes].reshape(
                n, padded, lanes
            )[:, :owned]

    def spread(step, carry):
        peer = lax.rem(me + 1 + lax.rem(step - 1 + n // 4, n - 1), n)
        pltpu.make_async_remote_copy(
            partial.at[peer], arrived.at[me], moment_send, moment_recv,
            device_id={"blk": peer}, device_id_type=MESH,
        ).start()
        return carry

    lax.fori_loop(1, n, spread, 0)
    pltpu.make_async_copy(partial.at[me], arrived.at[me], moment_recv).start()
    pltpu.make_async_copy(arrived, arrived, moment_recv).wait()
    moments = jnp.sum(arrived[...], axis=0)
    strengths = []
    for p in range(pieces):
        strength = jnp.zeros((owned, lanes), jnp.float32)
        for c in range(components):
            row = (c * pieces + p) * owned
            strength = strength + moments[row : row + owned] * moments[row : row + owned]
        strengths.append(strength)
    strength = jnp.concatenate(strengths, axis=1)
    out[...] = mask[...].astype(jnp.float32) * strength

    for chunk in range(chunks):
        pltpu.make_async_copy(
            final_in.at[chunk, pl.ds(0, n - 1)], final_in.at[chunk, pl.ds(0, n - 1)], send_sem.at[0, chunk]
        ).wait()
        if chunk < full:
            pltpu.make_async_copy(
                initial_in.at[chunk, pl.ds(0, n - 1)], initial_in.at[chunk, pl.ds(0, n - 1)], send_sem.at[1, chunk]
            ).wait()
    pltpu.make_async_copy(
        partial.at[pl.ds(0, n - 1)], partial.at[pl.ds(0, n - 1)], moment_send
    ).wait()


def on_device(n, initial_vectors, final_vectors, dipole, block_lengths, pair_mask):
    components, blocks, size, _ = dipole.shape
    owned, owned_final = initial_vectors.shape[0], final_vectors.shape[0]
    padded = (owned // 8 + 1) * 8
    full = -(-owned // (padded - owned))
    chunks = full + 1
    assert blocks % chunks == 0 and full * (padded - owned) == owned
    width = blocks // chunks * size
    return pl.pallas_call(
        functools.partial(kernel, n, chunks),
        out_shape=jax.ShapeDtypeStruct(pair_mask.shape, jnp.float32),
        in_specs=[
            pl.BlockSpec(memory_space=pl.ANY),
            pl.BlockSpec(memory_space=pl.ANY),
            pl.BlockSpec(memory_space=pl.ANY),
            pl.BlockSpec(memory_space=pltpu.SMEM),
            pl.BlockSpec(memory_space=pltpu.VMEM),
        ],
        out_specs=pl.BlockSpec(memory_space=pltpu.VMEM),
        scratch_shapes=[
            pltpu.VMEM(initial_vectors.shape, jnp.bfloat16),
            pltpu.VMEM((n, full, padded, width), jnp.bfloat16),
            pltpu.VMEM((chunks, n, owned_final, width), jnp.bfloat16),
            pltpu.VMEM((full, n, padded, width), jnp.bfloat16),
            pltpu.VMEM(dipole.shape, jnp.bfloat16),
            pltpu.VMEM((n, components * (n * owned_final // 128) * owned, 128), jnp.float32),
            pltpu.VMEM((n, components * (n * owned_final // 128) * owned, 128), jnp.float32),
            pltpu.SemaphoreType.DMA,
            pltpu.SemaphoreType.DMA,
            pltpu.SemaphoreType.DMA((2, chunks)),
            pltpu.SemaphoreType.DMA((chunks,)),
            pltpu.SemaphoreType.DMA((chunks,)),
            pltpu.SemaphoreType.DMA,
            pltpu.SemaphoreType.DMA,
            pltpu.SemaphoreType.REGULAR((2, 2)),
        ],
        compiler_params=pltpu.CompilerParams(
            collective_id=0, has_side_effects=True, vmem_limit_bytes=56 * 1024 * 1024
        ),
        cost_estimate=pl.CostEstimate(
            flops=2 * components * blocks * size * n * owned_final * (size + n * padded),
            bytes_accessed=2 * components * blocks * size * size + 4 * n * width * chunks * owned_final,
            transcendentals=0,
        ),
    )(initial_vectors, final_vectors, dipole, block_lengths, pair_mask)


def solution(mesh):
    placed = (
        P(("groups", "blk"), None),
        P(("groups", "blk"), None),
        P(None, ("groups", "blk"), None, None),
        P(("groups", "blk")),
        P(("groups", "blk"), None),
    )
    return jax.shard_map(
        functools.partial(on_device, mesh.shape["blk"]),
        mesh=mesh, in_specs=placed, out_specs=P(("groups", "blk"), None), check_vma=False,
    )
```
